32 devices in a mesh: grp: 8 (over y, x, core), seq: 4 (over z).
Axes of the slice: x: 2, y: 2, z: 4, core: 2. Of those that a mesh axis runs over, the one named last changes fastest.
Arguments:
- prompt_hidden: bfloat16 [8, 4096, 5120], P('grp', 'seq'), may hold values from -6 to 6
- resp_hidden: bfloat16 [8, 512, 5120], P('grp', 'seq'), may hold values from -6 to 6
- queries: bfloat16 [8, 512, 1024], P('grp', 'seq'), may hold values from -180 to 180
- grad_out: bfloat16 [8, 512, 1024], P('grp', 'seq'), may hold values from -6 to 6
- kv_weight: bfloat16 [5120, 256], P(('grp', 'seq')), may hold values from -0.078125 to 0.078125
- prompt_lengths: int32 [8], P('grp'), may hold values from 2048 to 4096
- response_lengths: int32 [8, 4], P('grp'), may hold values from 1 to 128, 320 in all within a row
Outputs:
- attended: bfloat16 [8, 512, 1024], P('grp', 'seq')
- query_grad: bfloat16 [8, 512, 1024], P('grp', 'seq')
- prompt_kv_grad: bfloat16 [8, 4096, 256], P('grp', 'seq')
- weight_grad: float32 [5120, 256], P(('grp', 'seq'))
The draws below stay inside these ranges and needn't reach their ends.
Inputs may be any that keep to these rules, and one draw needn't show every extreme that they name: `response_lengths`: every prompt has one response of exactly 128 live tokens.
All inputs are finite; a program needn't handle non-finite values.
Results may differ from the reference program's by a relative error of at most 0.025.
The reference program's roundings to bfloat16 on the way count: a program that leaves them out, or rounds other values in their place, can miss the bound.
Values may be sent and summed in bfloat16 or wider, within the bound.
A program may use at most 128 MiB of HBM per device.

```python
import math
import jax
import jax.numpy as jnp
import numpy as np
from jax import lax

D = 5120
DH = 128
HQ = 8
RT_DEV = 128
PROMPTS = 8
PLEN = 4096
RESP = 512
N_SEQ = 4


def draw_queries(key, part):
    key = jax.random.fold_in(key, 11)
    base = jnp.clip(jax.random.normal(key, (PROMPTS, RESP, HQ * DH), jnp.float32), -6.0, 6.0)
    return base.astype(jnp.bfloat16)


def plant(values, key, smallest, top_value):
    place = [jax.random.randint(jax.random.fold_in(key, axis), (), 0, length) for axis, length in enumerate(values.shape)]
    widest = values.shape.index(max(values.shape))
    beside = place[:widest] + [(place[widest] + 1) % values.shape[widest]] + place[widest + 1:]
    return values.at[tuple(place)].set(smallest).at[tuple(beside)].set(top_value)


def block_levels(own_key, extent, split, least, largest):
    def one(dim, shards_of):
        draws = jax.random.uniform(jax.random.fold_in(jax.random.fold_in(own_key, 6), dim), (shards_of,), jnp.float32, least / len(split), largest / len(split))
        return jnp.repeat(jnp.exp(draws), extent[dim] // shards_of).reshape((-1,) + (1,) * (len(extent) - dim - 1))

    level = one(*split[0])
    for cut in split[1:]:
        level = level * one(*cut)
    return level


def profile(count, total, bound, skew):
    weights = [(1 << 20) // math.isqrt(rank ** skew) + 1 for rank in range(2, count + 1)]
    spare, holding = total - bound - (count - 1), [1] * (count - 1)
    while spare > 0:
        movable = [i for i in range(count - 1) if holding[i] < bound]
        pool, left = sum([weights[i] for i in movable]), spare
        for i in movable:
            addition = min(bound - holding[i], max(1, left * weights[i] // pool), spare)
            holding[i] = holding[i] + addition
            spare = spare - addition
    return np.array([bound] + holding)


def uneven(key, amount, total, bound, slope):
    if amount == 2:
        one = jax.random.randint(key, (), max(1, total - bound), min(bound, total - 1) + 1)
        return jnp.stack([one, total - one])
    sizes = jnp.asarray(profile(amount, total, bound, slope), jnp.int32)
    couples = (amount - 1) // 2
    giver, taker = sizes[1:1 + 2 * couples:2], sizes[2:2 + 2 * couples:2]
    slack = jnp.minimum(giver - 1, bound - taker)
    shifted = jax.random.randint(jax.random.fold_in(key, 1), (couples,), 0, 1 << 20) % (slack + 1)
    sizes = sizes.at[1:1 + 2 * couples:2].set(giver - shifted).at[2:2 + 2 * couples:2].set(taker + shifted)
    return sizes[jax.random.permutation(jax.random.fold_in(key, 2), amount)]


def centred(key, dims, spread, reach, split=(), dtype=jnp.bfloat16):
    level = block_levels(key, dims, split, -0.22, 0.18) if split else 1.0
    result = jax.random.normal(key, dims, jnp.float32) * spread * level
    return jnp.minimum(jnp.maximum(result, -reach), reach).astype(dtype)


def setup_inputs(seed: int = 0) -> dict:
    streams_of = jax.random.split(jax.random.key(seed), 8)
    return {
        "prompt_hidden": centred(streams_of[0], (PROMPTS, PLEN, D), 1.0, 6.0, ((0, 8), (1, 4))),
        "resp_hidden": centred(streams_of[1], (PROMPTS, RESP, D), 1.0, 6.0, ((0, 8), (1, 4))),
        "queries": draw_queries(jax.random.fold_in(streams_of[7], 71), 0),
        "grad_out": centred(streams_of[3], (PROMPTS, RESP, HQ * DH), 1.0, 6.0, ((0, 8), (1, 4))),
        "kv_weight": centred(streams_of[4], (D, 2 * DH), D ** -0.5, 0.078125, ((0, 32),)),
        "prompt_lengths": plant(jax.random.randint(streams_of[5], (PROMPTS,), PLEN // 2, PLEN + 1), jax.random.fold_in(streams_of[5], 1), PLEN // 2, PLEN).astype(jnp.int32),
        "response_lengths": jax.vmap(lambda own: uneven(own, N_SEQ, N_SEQ * RT_DEV * 5 // 8, RT_DEV, 2))(jax.random.split(streams_of[6], PROMPTS)).reshape((PROMPTS, N_SEQ)).astype(jnp.int32),
    }


def respond(q_rows, grad_rows, prompt_kv, resp_kv, prompt_len, resp_len):
    slots = q_rows.shape[0]
    plen_all = prompt_kv.shape[0]
    scale = DH ** -0.5
    keys = jnp.concatenate([prompt_kv[:, :DH], resp_kv[:, :DH]], 0).astype(jnp.float32)
    values = jnp.concatenate([prompt_kv[:, DH:], resp_kv[:, DH:]], 0).astype(jnp.float32)
    position = jnp.arange(slots)
    live = position < resp_len
    prompt_ok = jnp.arange(plen_all) < prompt_len
    allowed = jnp.concatenate([jnp.broadcast_to(prompt_ok[None, :], (slots, plen_all)), position[None, :] <= position[:, None]], 1)
    grad_live = jnp.where(live[:, None], grad_rows, jnp.zeros_like(grad_rows))
    q_heads = q_rows.reshape(slots, HQ, DH).astype(jnp.float32)
    g_heads = grad_live.reshape(slots, HQ, DH).astype(jnp.float32)
    scores = jnp.einsum('thd,kd->htk', q_heads, keys) * scale
    scores = jnp.where(allowed[None], scores, -jnp.inf)
    top = jnp.max(scores, 2, keepdims=True)
    expo = jnp.exp(scores - top)
    probs = expo / jnp.sum(expo, 2, keepdims=True)
    probs_b = lax.optimization_barrier(probs.astype(jnp.bfloat16)).astype(jnp.float32)
    attended = jnp.einsum('htk,kd->thd', probs_b, values)
    attended = jnp.where(live[:, None, None], attended, jnp.zeros_like(attended)).astype(jnp.bfloat16)
    delta = jnp.sum(g_heads * attended.astype(jnp.float32), 2).T
    dprob = jnp.einsum('thd,kd->htk', g_heads, values)
    dscore = probs * (dprob - delta[:, :, None]) * scale
    dscore = lax.optimization_barrier(dscore.astype(jnp.bfloat16)).astype(jnp.float32)
    query_grad = jnp.einsum('htk,kd->thd', dscore, keys).astype(jnp.bfloat16)
    key_grad = jnp.einsum('htk,thd->kd', dscore, q_heads)
    value_grad = jnp.einsum('htk,thd->kd', probs_b, g_heads)
    kv_grad = jnp.concatenate([key_grad, value_grad], 1)
    return attended.reshape(slots, HQ * DH), query_grad.reshape(slots, HQ * DH), kv_grad[:plen_all], kv_grad[plen_all:]


def reference(prompt_hidden, resp_hidden, queries, grad_out, kv_weight, prompt_lengths, response_lengths):
    def one_group(items):
        hidden_p, hidden_r, q_group, g_group, prompt_len, lengths_row = items
        prompt_kv = jnp.dot(hidden_p, kv_weight, preferred_element_type=jnp.float32).astype(jnp.bfloat16)
        resp_kv = jnp.dot(hidden_r, kv_weight, preferred_element_type=jnp.float32).astype(jnp.bfloat16)

        def one_resp(pieces):
            q_rows, g_rows, kv_rows, resp_len = pieces
            return respond(q_rows, g_rows, prompt_kv, kv_rows, prompt_len, resp_len)

        attended, query_grad, prompt_parts, resp_grad = lax.map(one_resp, (
            q_group.reshape(N_SEQ, RT_DEV, HQ * DH), g_group.reshape(N_SEQ, RT_DEV, HQ * DH),
            resp_kv.reshape(N_SEQ, RT_DEV, 2 * DH), lengths_row))
        prompt_grad = jnp.sum(prompt_parts, 0).astype(jnp.bfloat16)
        resp_grad = resp_grad.reshape(RESP, 2 * DH).astype(jnp.bfloat16)
        weight_part = jnp.dot(hidden_p.T, prompt_grad, preferred_element_type=jnp.float32)
        weight_part = weight_part + jnp.dot(hidden_r.T, resp_grad, preferred_element_type=jnp.float32)
        return attended.reshape(RESP, HQ * DH), query_grad.reshape(RESP, HQ * DH), prompt_grad, weight_part

    attended, query_grad, prompt_kv_grad, weight_parts = lax.map(one_group, (
        prompt_hidden, resp_hidden, queries, grad_out, prompt_lengths, response_lengths))
    weight_grad = jnp.sum(weight_parts, 0)
    return attended, query_grad, prompt_kv_grad, weight_grad
```

```python
import functools

import jax
import jax.numpy as jnp
from jax import lax
from jax.experimental import pallas as pl
from jax.experimental.pallas import tpu as pltpu
from jax.sharding import PartitionSpec as P

MESH = pl.DeviceIdType.MESH
CORES = 2


def place(cols):
    grp = lax.axis_index("grp")
    seq = lax.axis_index("seq")
    return grp, seq, grp // CORES, grp % CORES


def greet(cols, seqs):
    grp, seq, col, core = place(cols)
    barrier = pltpu.get_barrier_semaphore()
    peers = [(grp, (seq + k) % seqs) for k in range(1, seqs)]
    peers += [(((col + j) % cols) * CORES + core, seq) for j in range(1, cols)]
    peers += [(col * CORES + 1 - core, seq)]
    for peer in peers:
        pl.semaphore_signal(barrier, inc=1, device_id=peer, device_id_type=MESH)
    pl.semaphore_wait(barrier, len(peers))


def remote(src, dst, send, recv, device):
    return pltpu.make_async_remote_copy(
        src_ref=src, dst_ref=dst, send_sem=send, recv_sem=recv, device_id=device, device_id_type=MESH
    )


def gather_kernel(cols, seqs, w_ref, out_ref, zs, zr, xs, xr, cs, cr, own_sem):
    grp, seq, col, core = place(cols)
    sibling = (col * CORES + 1 - core, seq)
    greet(cols, seqs)
    own = pltpu.make_async_copy(w_ref.at[0], out_ref.at[grp * seqs + seq], own_sem)
    own.start()
    sent = []
    for k in range(1, seqs):
        copy = remote(
            w_ref.at[0], out_ref.at[grp * seqs + seq], zs.at[k - 1], zr.at[k - 1], (grp, (seq + k) % seqs)
        )
        copy.start()
        sent.append(copy)
    first = list(sent)
    across = {}
    over = []
    for k in range(seqs):
        if k:
            first[k - 1].wait_recv()
        index = grp * seqs + (seq + seqs - k) % seqs
        src = w_ref.at[0] if k == 0 else out_ref.at[index]
        for j in range(1, cols):
            copy = remote(
                src, out_ref.at[index], xs.at[k, j - 1], xr.at[k, j - 1], (((col + j) % cols) * CORES + core, seq)
            )
            copy.start()
            across[k, j] = copy
        copy = remote(src, out_ref.at[index], cs.at[k, 0], cr.at[k, 0], sibling)
        copy.start()
        over.append(copy)
    for k in range(seqs):
        for j in range(1, cols):
            across[k, j].wait_recv()
            index = (((col + cols - j) % cols) * CORES + core) * seqs + (seq + seqs - k) % seqs
            copy = remote(out_ref.at[index], out_ref.at[index], cs.at[k, j], cr.at[k, j], sibling)
            copy.start()
            over.append(copy)
    for copy in over:
        copy.wait_recv()
    for copy in sent + list(across.values()) + over:
        copy.wait_send()
    own.wait()


def gather_weight(weight, cols, seqs):
    rows, width = weight.shape
    out = pl.pallas_call(
        functools.partial(gather_kernel, cols, seqs),
        out_shape=jax.ShapeDtypeStruct((cols * CORES * seqs, rows, width), weight.dtype),
        in_specs=[pl.BlockSpec(memory_space=pl.ANY)],
        out_specs=pl.BlockSpec(memory_space=pl.ANY),
        scratch_shapes=[
            pltpu.SemaphoreType.DMA((seqs - 1,)),
            pltpu.SemaphoreType.DMA((seqs - 1,)),
            pltpu.SemaphoreType.DMA((seqs, cols - 1)),
            pltpu.SemaphoreType.DMA((seqs, cols - 1)),
            pltpu.SemaphoreType.DMA((seqs, cols)),
            pltpu.SemaphoreType.DMA((seqs, cols)),
            pltpu.SemaphoreType.DMA,
        ],
        compiler_params=pltpu.CompilerParams(collective_id=0, has_side_effects=True),
        name="gather_weight",
    )(weight[None])
    return out.reshape(cols * CORES * seqs * rows, width)


def finish_kernel(
    cols, seqs, part_ref, rgrad_ref, x_ref, xr_ref, pgrad_ref, wgrad_ref,
    xbuf, gt, ksend, krecv, pair, crecv, xsend, xrecv, total, zsend, zrecv,
    xsem, ks, kr, cs, cr, xs, xr, zs, zr,
):
    grp, seq, col, core = place(cols)
    sibling = (col * CORES + 1 - core, seq)
    plen, width = pgrad_ref.shape
    rt = rgrad_ref.shape[0]
    block = pair.shape[1]
    half = block // CORES
    rows = wgrad_ref.shape[0]
    loads = []
    for j in range(cols):
        at = pl.ds(pl.multiple_of(((col + j) % cols) * block, 128), block)
        loads.append(pltpu.make_async_copy(x_ref.at[:, at], xbuf.at[j, pl.ds(0, plen)], xsem.at[0, j]))
        loads.append(pltpu.make_async_copy(xr_ref.at[:, at], xbuf.at[j, pl.ds(plen, rt)], xsem.at[1, j]))
    for load in loads:
        load.start()
    greet(cols, seqs)

    sends = []
    for k in range(1, seqs):
        ksend[k - 1] = part_ref[(seq + k) % seqs].astype(jnp.bfloat16)
        copy = remote(
            ksend.at[k - 1], krecv.at[k - 1], ks.at[k - 1], kr.at[k - 1], (grp, (seq + k) % seqs)
        )
        copy.start()
        sends.append(copy)
    gt[:, pl.ds(plen, rt)] = rgrad_ref[...].astype(jnp.float32).T.astype(jnp.bfloat16)
    for load in loads:
        load.wait()
    for copy in sends:
        copy.wait_recv()
    for t in range(0, plen, 256):
        at = pl.ds(t, 256)
        acc = part_ref[seq, at, :]
        for k in range(1, seqs):
            acc = acc + krecv[k - 1, at, :].astype(jnp.float32)
        grad = acc.astype(jnp.bfloat16)
        pgrad_ref[at, :] = grad
        gt[:, at] = grad.astype(jnp.float32).T.astype(jnp.bfloat16)

    tile = 256 if block % 256 == 0 else 128
    mine = pl.ds(pl.multiple_of(core * half, 8), half)
    other = pl.ds(pl.multiple_of((1 - core) * half, 8), half)
    order = list(range(1, cols)) + [0]
    over, across = {}, {}

    def forward(j):
        over[j].wait_recv()
        xsend[j - 1] = (pair[j, mine, :] + crecv[j]).astype(jnp.bfloat16)
        copy = remote(
            xsend.at[j - 1], xrecv.at[j - 1], xs.at[j - 1], xr.at[j - 1],
            (((col + j) % cols) * CORES + core, seq),
        )
        copy.start()
        across[j] = copy

    for step, j in enumerate(order):
        for t in range(0, block, tile):
            at = pl.ds(t, tile)
            prod = jnp.dot(gt[...], xbuf[j, :, at], preferred_element_type=jnp.float32)
            pair[j, at, :] = prod.T
        copy = remote(pair.at[j, other], crecv.at[j], cs.at[j], cr.at[j], sibling)
        copy.start()
        over[j] = copy
        if step:
            forward(order[step - 1])
    over[0].wait_recv()
    total[...] = pair[0, mine, :] + crecv[0]
    for j in range(1, cols):
        across[j].wait_recv()
        total[...] += xrecv[j - 1].astype(jnp.float32)

    last = []
    for k in range(1, seqs):
        at = pl.ds(pl.multiple_of(((seq + k) % seqs) * rows, 8), rows)
        zsend[k - 1] = total[at, :].astype(jnp.bfloat16)
        copy = remote(
            zsend.at[k - 1], zrecv.at[k - 1], zs.at[k - 1], zr.at[k - 1], (grp, (seq + k) % seqs)
        )
        copy.start()
        last.append(copy)
    acc = total[pl.ds(pl.multiple_of(seq * rows, 8), rows), :]
    for k in range(1, seqs):
        last[k - 1].wait_recv()
        acc = acc + zrecv[k - 1].astype(jnp.float32)
    wgrad_ref[...] = acc
    for copy in sends + list(over.values()) + list(across.values()) + last:
        copy.wait_send()


def finish(part, rgrad, x, xr, cols, seqs):
    plen, d = x.shape
    rt = xr.shape[0]
    width = part.shape[-1]
    block = d // cols
    half = block // CORES
    rows = half // seqs
    bf16, f32 = jnp.bfloat16, jnp.float32
    vmem = pl.BlockSpec(memory_space=pltpu.VMEM)
    hbm = pl.BlockSpec(memory_space=pl.ANY)
    dma = pltpu.SemaphoreType.DMA
    return pl.pallas_call(
        functools.partial(finish_kernel, cols, seqs),
        out_shape=(
            jax.ShapeDtypeStruct((plen, width), bf16),
            jax.ShapeDtypeStruct((rows, width), f32),
        ),
        in_specs=[vmem, vmem, hbm, hbm],
        out_specs=(vmem, vmem),
        scratch_shapes=[
            pltpu.VMEM((cols, plen + rt, block), bf16),
            pltpu.VMEM((width, plen + rt), bf16),
            pltpu.VMEM((seqs - 1, plen, width), bf16),
            pltpu.VMEM((seqs - 1, plen, width), bf16),
            pltpu.VMEM((cols, block, width), f32),
            pltpu.VMEM((cols, half, width), f32),
            pltpu.VMEM((cols - 1, half, width), bf16),
            pltpu.VMEM((cols - 1, half, width), bf16),
            pltpu.VMEM((half, width), f32),
            pltpu.VMEM((seqs - 1, rows, width), bf16),
            pltpu.VMEM((seqs - 1, rows, width), bf16),
            dma((2, cols)),
            dma((seqs - 1,)), dma((seqs - 1,)),
            dma((cols,)), dma((cols,)),
            dma((cols - 1,)), dma((cols - 1,)),
            dma((seqs - 1,)), dma((seqs - 1,)),
        ],
        compiler_params=pltpu.CompilerParams(
            collective_id=1, has_side_effects=True, vmem_limit_bytes=52 * 2**20
        ),
        name="finish",
    )(part, rgrad, x, xr)


def per_device(
    cols, seqs,
    prompt_hidden, resp_hidden, queries, grad_out, kv_weight, prompt_lengths, response_lengths
):
    seq_rank = lax.axis_index("seq")
    head_dim = kv_weight.shape[1] // 2
    rt_dev = resp_hidden.shape[1]
    width = queries.shape[2]
    heads = width // head_dim
    group_heads = 2
    blocks = heads // group_heads
    scale = head_dim ** (-0.5)
    prompt_rows = prompt_hidden[0]
    resp_rows = resp_hidden[0]
    piece = gather_weight(kv_weight, cols, seqs)
    own_kv = jnp.dot(prompt_rows, piece, preferred_element_type=jnp.float32)
    resp_kv = jnp.dot(resp_rows, piece, preferred_element_type=jnp.float32)
    own_kv = own_kv.astype(jnp.bfloat16)
    resp_kv = resp_kv.astype(jnp.bfloat16)
    prompt_kv = lax.all_gather(own_kv, "seq", axis=0, tiled=True)
    plen_all = prompt_kv.shape[0]
    prompt_len = prompt_lengths[0]
    lengths_row = response_lengths[0]
    members = jnp.arange(lengths_row.shape[0])
    resp_len = jnp.sum(jnp.where(members == seq_rank, lengths_row, 0))
    position = jnp.arange(rt_dev)
    live = position < resp_len
    prompt_ok = jnp.arange(plen_all) < prompt_len
    allowed = jnp.concatenate(
        [
            jnp.broadcast_to(prompt_ok[None, :], (rt_dev, plen_all)),
            position[None, :] <= position[:, None],
        ],
        1,
    )
    keys = jnp.concatenate([prompt_kv[:, :head_dim], resp_kv[:, :head_dim]], 0)
    values = jnp.concatenate([prompt_kv[:, head_dim:], resp_kv[:, head_dim:]], 0)
    grad_live = jnp.where(live[:, None], grad_out[0], jnp.zeros_like(grad_out[0]))
    q_blocks = queries[0].reshape(rt_dev, blocks, group_heads, head_dim).transpose(1, 0, 2, 3)
    g_blocks = grad_live.reshape(rt_dev, blocks, group_heads, head_dim).transpose(1, 0, 2, 3)

    def attend_block(pieces):
        q_part, g_part = pieces
        scores = jnp.einsum("thd,kd->htk", q_part, keys, preferred_element_type=jnp.float32) * scale
        scores = jnp.where(allowed[None], scores, -jnp.inf)
        top = jnp.max(scores, 2, keepdims=True)
        expo = jnp.exp(scores - top)
        total = jnp.sum(expo, 2, keepdims=True)
        probs = expo / total
        probs_b = probs.astype(jnp.bfloat16)
        out_part = jnp.einsum("htk,kd->thd", probs_b, values, preferred_element_type=jnp.float32)
        out_part = jnp.where(live[:, None, None], out_part, jnp.zeros_like(out_part)).astype(
            jnp.bfloat16
        )
        delta = jnp.sum(g_part.astype(jnp.float32) * out_part.astype(jnp.float32), 2).T
        dprob = jnp.einsum("thd,kd->htk", g_part, values, preferred_element_type=jnp.float32)
        dscore = (probs * (dprob - delta[:, :, None]) * scale).astype(jnp.bfloat16)
        q_grad = jnp.einsum("htk,kd->thd", dscore, keys, preferred_element_type=jnp.float32).astype(
            jnp.bfloat16
        )
        key_grad = jnp.einsum("htk,thd->kd", dscore, q_part, preferred_element_type=jnp.float32)
        value_grad = jnp.einsum("htk,thd->kd", probs_b, g_part, preferred_element_type=jnp.float32)
        return (out_part, q_grad, key_grad, value_grad)

    out_b, qg_b, key_grad, value_grad = lax.map(attend_block, (q_blocks, g_blocks))
    attended = out_b.transpose(1, 0, 2, 3).reshape(rt_dev, width)
    query_grad = qg_b.transpose(1, 0, 2, 3).reshape(rt_dev, width)
    kv_grad = jnp.concatenate([jnp.sum(key_grad, 0), jnp.sum(value_grad, 0)], 1)
    resp_grad = kv_grad[plen_all:].astype(jnp.bfloat16)
    part = kv_grad[:plen_all].reshape(seqs, plen_all // seqs, 2 * head_dim)
    prompt_grad, weight_grad = finish(part, resp_grad, prompt_rows, resp_rows, cols, seqs)
    return (attended[None], query_grad[None], prompt_grad[None], weight_grad)


def solution(mesh):
    cols, seqs = mesh.shape["grp"] // CORES, mesh.shape["seq"]
    return jax.shard_map(
        functools.partial(per_device, cols, seqs),
        mesh=mesh,
        in_specs=(
            P("grp", "seq", None),
            P("grp", "seq", None),
            P("grp", "seq", None),
            P("grp", "seq", None),
            P(("grp", "seq"), None),
            P("grp"),
            P("grp", None),
        ),
        out_specs=(
            P("grp", "seq", None),
            P("grp", "seq", None),
            P("grp", "seq", None),
            P(("grp", "seq"), None),
        ),
        check_vma=False,
    )
```

```python
import functools
import math

import jax
import jax.numpy as jnp
from jax import lax
from jax.experimental import pallas as pl
from jax.experimental.pallas import tpu as pltpu
from jax.sharding import PartitionSpec as P

MESH = pl.DeviceIdType.MESH
CORES = 2


def place(cols):
    grp = lax.axis_index("grp")
    seq = lax.axis_index("seq")
    return grp, seq, grp // CORES, grp % CORES


def greet(cols, seqs):
    grp, seq, col, core = place(cols)
    barrier = pltpu.get_barrier_semaphore()
    peers = [(grp, (seq + k) % seqs) for k in range(1, seqs)]
    peers += [(((col + j) % cols) * CORES + core, seq) for j in range(1, cols)]
    peers += [(col * CORES + 1 - core, seq)]
    for peer in peers:
        pl.semaphore_signal(barrier, inc=1, device_id=peer, device_id_type=MESH)
    pl.semaphore_wait(barrier, len(peers))


def remote(src, dst, send, recv, device):
    return pltpu.make_async_remote_copy(
        src_ref=src, dst_ref=dst, send_sem=send, recv_sem=recv, device_id=device, device_id_type=MESH
    )


def encode(x, group):
    rows, width = x.shape
    parts = x.reshape(rows // group, group, width)
    top = jnp.maximum(jnp.max(jnp.abs(parts), 1, keepdims=True), 1e-33)
    code = jnp.floor(parts * (32000.0 / top) + 0.5).astype(jnp.int32)
    return code.reshape(rows, width).astype(jnp.int16), (top * (1.0 / 32000.0)).reshape(rows // group, width)


def decode(code, scale):
    rows, width = code.shape
    groups = scale.shape[0]
    parts = code.astype(jnp.int32).astype(jnp.float32).reshape(groups, rows // groups, width)
    return (parts * scale.reshape(groups, 1, width)).reshape(rows, width)


class Pair:
    def __init__(self, codes, scales, sends, recvs, index, device):
        self.copies = [
            remote(src.at[index], dst.at[index], sends.at[i, index], recvs.at[i, index], device)
            for i, (src, dst) in enumerate((codes, scales))
        ]

    def start(self):
        for copy in self.copies:
            copy.start()

    def wait_recv(self):
        for copy in self.copies:
            copy.wait_recv()

    def wait_send(self):
        for copy in self.copies:
            copy.wait_send()


def gather_kernel(cols, seqs, w_ref, out_ref, zs, zr, xs, xr, cs, cr, own_sem):
    grp, seq, col, core = place(cols)
    sibling = (col * CORES + 1 - core, seq)
    greet(cols, seqs)
    own = pltpu.make_async_copy(w_ref.at[0], out_ref.at[grp * seqs + seq], own_sem)
    own.start()
    sent = []
    for k in range(1, seqs):
        copy = remote(
            w_ref.at[0], out_ref.at[grp * seqs + seq], zs.at[k - 1], zr.at[k - 1], (grp, (seq + k) % seqs)
        )
        copy.start()
        sent.append(copy)
    first = list(sent)
    across = {}
    over = []
    for k in range(seqs):
        if k:
            first[k - 1].wait_recv()
        index = grp * seqs + (seq + seqs - k) % seqs
        src = w_ref.at[0] if k == 0 else out_ref.at[index]
        for j in range(1, cols):
            copy = remote(
                src, out_ref.at[index], xs.at[k, j - 1], xr.at[k, j - 1], (((col + j) % cols) * CORES + core, seq)
            )
            copy.start()
            across[k, j] = copy
        copy = remote(src, out_ref.at[index], cs.at[k, 0], cr.at[k, 0], sibling)
        copy.start()
        over.append(copy)
    for k in range(seqs):
        for j in range(1, cols):
            across[k, j].wait_recv()
            index = (((col + cols - j) % cols) * CORES + core) * seqs + (seq + seqs - k) % seqs
            copy = remote(out_ref.at[index], out_ref.at[index], cs.at[k, j], cr.at[k, j], sibling)
            copy.start()
            over.append(copy)
    for copy in over:
        copy.wait_recv()
    for copy in sent + list(across.values()) + over:
        copy.wait_send()
    own.wait()


def gather_weight(weight, cols, seqs):
    rows, width = weight.shape
    out = pl.pallas_call(
        functools.partial(gather_kernel, cols, seqs),
        out_shape=jax.ShapeDtypeStruct((cols * CORES * seqs, rows, width), weight.dtype),
        in_specs=[pl.BlockSpec(memory_space=pl.ANY)],
        out_specs=pl.BlockSpec(memory_space=pl.ANY),
        scratch_shapes=[
            pltpu.SemaphoreType.DMA((seqs - 1,)),
            pltpu.SemaphoreType.DMA((seqs - 1,)),
            pltpu.SemaphoreType.DMA((seqs, cols - 1)),
            pltpu.SemaphoreType.DMA((seqs, cols - 1)),
            pltpu.SemaphoreType.DMA((seqs, cols)),
            pltpu.SemaphoreType.DMA((seqs, cols)),
            pltpu.SemaphoreType.DMA,
        ],
        compiler_params=pltpu.CompilerParams(collective_id=0, has_side_effects=True),
        name="gather_weight",
    )(weight[None])
    return out.reshape(cols * CORES * seqs * rows, width)


def finish_kernel(
    cols, seqs, part_ref, rgrad_ref, x_ref, xr_ref, pgrad_ref, wgrad_ref,
    xbuf, gt, ksend, krecv, kscale, kscaled, pair, crecv, xsend, xrecv, xscale, xscaled,
    total, zsend, zrecv, zscale, zscaled,
    xsem, ks, kr, cs, cr, xs, xr, zs, zr,
):
    grp, seq, col, core = place(cols)
    sibling = (col * CORES + 1 - core, seq)
    plen, width = pgrad_ref.shape
    rt = rgrad_ref.shape[0]
    block = pair.shape[1]
    half = block // CORES
    rows = wgrad_ref.shape[0]
    loads = []
    for j in range(cols):
        at = pl.ds(pl.multiple_of(((col + j) % cols) * block, 128), block)
        loads.append(pltpu.make_async_copy(x_ref.at[:, at], xbuf.at[j, pl.ds(0, plen)], xsem.at[0, j]))
        loads.append(pltpu.make_async_copy(xr_ref.at[:, at], xbuf.at[j, pl.ds(plen, rt)], xsem.at[1, j]))
    for load in loads:
        load.start()
    greet(cols, seqs)

    sends = []
    for k in range(1, seqs):
        for t in range(0, plen, 512):
            ksend[k - 1, pl.ds(t, 512)], kscale[k - 1, pl.ds(t // 64, 8)] = encode(
                part_ref[(seq + k) % seqs, pl.ds(t, 512)], 64
            )
        copy = Pair(
            (ksend, krecv), (kscale, kscaled), ks, kr, k - 1, (grp, (seq + k) % seqs)
        )
        copy.start()
        sends.append(copy)
    gt[:, pl.ds(plen, rt)] = rgrad_ref[...].astype(jnp.float32).T.astype(jnp.bfloat16)
    for load in loads:
        load.wait()
    for copy in sends:
        copy.wait_recv()
    for t in range(0, plen, 512):
        at = pl.ds(t, 512)
        acc = part_ref[seq, at, :]
        for k in range(1, seqs):
            acc = acc + decode(krecv[k - 1, at, :], kscaled[k - 1, pl.ds(t // 64, 8)])
        grad = acc.astype(jnp.bfloat16)
        pgrad_ref[at, :] = grad
        gt[:, at] = grad.astype(jnp.float32).T.astype(jnp.bfloat16)

    tile = 256 if block % 256 == 0 else 128
    mine = pl.ds(pl.multiple_of(core * half, 8), half)
    other = pl.ds(pl.multiple_of((1 - core) * half, 8), half)
    order = list(range(1, cols)) + [0]
    over, across = {}, {}

    def forward(j):
        over[j].wait_recv()
        xsend[j - 1], xscale[j - 1] = encode(pair[j, mine, :] + crecv[j], 64)
        copy = Pair(
            (xsend, xrecv), (xscale, xscaled), xs, xr, j - 1, (((col + j) % cols) * CORES + core, seq)
        )
        copy.start()
        across[j] = copy

    for step, j in enumerate(order):
        for t in range(0, block, tile):
            at = pl.ds(t, tile)
            prod = jnp.dot(gt[...], xbuf[j, :, at], preferred_element_type=jnp.float32)
            pair[j, at, :] = prod.T
        copy = remote(pair.at[j, other], crecv.at[j], cs.at[j], cr.at[j], sibling)
        copy.start()
        over[j] = copy
        if step:
            forward(order[step - 1])
    over[0].wait_recv()
    total[...] = pair[0, mine, :] + crecv[0]
    for j in range(1, cols):
        across[j].wait_recv()
        total[...] += decode(xrecv[j - 1], xscaled[j - 1])

    last = []
    for k in range(1, seqs):
        at = pl.ds(pl.multiple_of(((seq + k) % seqs) * rows, 8), rows)
        zsend[k - 1], zscale[k - 1] = encode(total[at, :], math.gcd(rows, 32))
        copy = Pair(
            (zsend, zrecv), (zscale, zscaled), zs, zr, k - 1, (grp, (seq + k) % seqs)
        )
        copy.start()
        last.append(copy)
    acc = total[pl.ds(pl.multiple_of(seq * rows, 8), rows), :]
    for k in range(1, seqs):
        last[k - 1].wait_recv()
        acc = acc + decode(zrecv[k - 1], zscaled[k - 1])
    wgrad_ref[...] = acc
    for copy in sends + list(over.values()) + list(across.values()) + last:
        copy.wait_send()


def finish(part, rgrad, x, xr, cols, seqs):
    plen, d = x.shape
    rt = xr.shape[0]
    width = part.shape[-1]
    block = d // cols
    half = block // CORES
    rows = half // seqs
    bf16, f32, i16 = jnp.bfloat16, jnp.float32, jnp.int16
    vmem = pl.BlockSpec(memory_space=pltpu.VMEM)
    hbm = pl.BlockSpec(memory_space=pl.ANY)
    dma = pltpu.SemaphoreType.DMA
    return pl.pallas_call(
        functools.partial(finish_kernel, cols, seqs),
        out_shape=(
            jax.ShapeDtypeStruct((plen, width), bf16),
            jax.ShapeDtypeStruct((rows, width), f32),
        ),
        in_specs=[vmem, vmem, hbm, hbm],
        out_specs=(vmem, vmem),
        scratch_shapes=[
            pltpu.VMEM((cols, plen + rt, block), bf16),
            pltpu.VMEM((width, plen + rt), bf16),
            pltpu.VMEM((seqs - 1, plen, width), i16),
            pltpu.VMEM((seqs - 1, plen, width), i16),
            pltpu.VMEM((seqs - 1, plen // 64, width), f32),
            pltpu.VMEM((seqs - 1, plen // 64, width), f32),
            pltpu.VMEM((cols, block, width), f32),
            pltpu.VMEM((cols, half, width), f32),
            pltpu.VMEM((cols - 1, half, width), i16),
            pltpu.VMEM((cols - 1, half, width), i16),
            pltpu.VMEM((cols - 1, half // 64, width), f32),
            pltpu.VMEM((cols - 1, half // 64, width), f32),
            pltpu.VMEM((half, width), f32),
            pltpu.VMEM((seqs - 1, rows, width), i16),
            pltpu.VMEM((seqs - 1, rows, width), i16),
            pltpu.VMEM((seqs - 1, rows // math.gcd(rows, 32), width), f32),
            pltpu.VMEM((seqs - 1, rows // math.gcd(rows, 32), width), f32),
            dma((2, cols)),
            dma((2, seqs - 1)), dma((2, seqs - 1)),
            dma((cols,)), dma((cols,)),
            dma((2, cols - 1)), dma((2, cols - 1)),
            dma((2, seqs - 1)), dma((2, seqs - 1)),
        ],
        compiler_params=pltpu.CompilerParams(
            collective_id=1, has_side_effects=True, vmem_limit_bytes=52 * 2**20
        ),
        name="finish",
    )(part, rgrad, x, xr)


def per_device(
    cols, seqs,
    prompt_hidden, resp_hidden, queries, grad_out, kv_weight, prompt_lengths, response_lengths
):
    seq_rank = lax.axis_index("seq")
    head_dim = kv_weight.shape[1] // 2
    rt_dev = resp_hidden.shape[1]
    width = queries.shape[2]
    heads = width // head_dim
    group_heads = 2
    blocks = heads // group_heads
    scale = head_dim ** (-0.5)
    prompt_rows = prompt_hidden[0]
    resp_rows = resp_hidden[0]
    piece = gather_weight(kv_weight, cols, seqs)
    own_kv = jnp.dot(prompt_rows, piece, preferred_element_type=jnp.float32)
    resp_kv = jnp.dot(resp_rows, piece, preferred_element_type=jnp.float32)
    own_kv = own_kv.astype(jnp.bfloat16)
    resp_kv = resp_kv.astype(jnp.bfloat16)
    prompt_kv = lax.all_gather(own_kv, "seq", axis=0, tiled=True)
    plen_all = prompt_kv.shape[0]
    prompt_len = prompt_lengths[0]
    lengths_row = response_lengths[0]
    members = jnp.arange(lengths_row.shape[0])
    resp_len = jnp.sum(jnp.where(members == seq_rank, lengths_row, 0))
    position = jnp.arange(rt_dev)
    live = position < resp_len
    prompt_ok = jnp.arange(plen_all) < prompt_len
    allowed = jnp.concatenate(
        [
            jnp.broadcast_to(prompt_ok[None, :], (rt_dev, plen_all)),
            position[None, :] <= position[:, None],
        ],
        1,
    )
    keys = jnp.concatenate([prompt_kv[:, :head_dim], resp_kv[:, :head_dim]], 0)
    values = jnp.concatenate([prompt_kv[:, head_dim:], resp_kv[:, head_dim:]], 0)
    grad_live = jnp.where(live[:, None], grad_out[0], jnp.zeros_like(grad_out[0]))
    q_blocks = queries[0].reshape(rt_dev, blocks, group_heads, head_dim).transpose(1, 0, 2, 3)
    g_blocks = grad_live.reshape(rt_dev, blocks, group_heads, head_dim).transpose(1, 0, 2, 3)

    def attend_block(pieces):
        q_part, g_part = pieces
        scores = jnp.einsum("thd,kd->htk", q_part, keys, preferred_element_type=jnp.float32) * scale
        scores = jnp.where(allowed[None], scores, -jnp.inf)
        top = jnp.max(scores, 2, keepdims=True)
        expo = jnp.exp(scores - top)
        total = jnp.sum(expo, 2, keepdims=True)
        probs = expo / total
        probs_b = probs.astype(jnp.bfloat16)
        out_part = jnp.einsum("htk,kd->thd", probs_b, values, preferred_element_type=jnp.float32)
        out_part = jnp.where(live[:, None, None], out_part, jnp.zeros_like(out_part)).astype(
            jnp.bfloat16
        )
        delta = jnp.sum(g_part.astype(jnp.float32) * out_part.astype(jnp.float32), 2).T
        dprob = jnp.einsum("thd,kd->htk", g_part, values, preferred_element_type=jnp.float32)
        dscore = (probs * (dprob - delta[:, :, None]) * scale).astype(jnp.bfloat16)
        q_grad = jnp.einsum("htk,kd->thd", dscore, keys, preferred_element_type=jnp.float32).astype(
            jnp.bfloat16
        )
        key_grad = jnp.einsum("htk,thd->kd", dscore, q_part, preferred_element_type=jnp.float32)
        value_grad = jnp.einsum("htk,thd->kd", probs_b, g_part, preferred_element_type=jnp.float32)
        return (out_part, q_grad, key_grad, value_grad)

    out_b, qg_b, key_grad, value_grad = lax.map(attend_block, (q_blocks, g_blocks))
    attended = out_b.transpose(1, 0, 2, 3).reshape(rt_dev, width)
    query_grad = qg_b.transpose(1, 0, 2, 3).reshape(rt_dev, width)
    kv_grad = jnp.concatenate([jnp.sum(key_grad, 0), jnp.sum(value_grad, 0)], 1)
    resp_grad = kv_grad[plen_all:].astype(jnp.bfloat16)
    part = kv_grad[:plen_all].reshape(seqs, plen_all // seqs, 2 * head_dim)
    prompt_grad, weight_grad = finish(part, resp_grad, prompt_rows, resp_rows, cols, seqs)
    return (attended[None], query_grad[None], prompt_grad[None], weight_grad)


def solution(mesh):
    cols, seqs = mesh.shape["grp"] // CORES, mesh.shape["seq"]
    return jax.shard_map(
        functools.partial(per_device, cols, seqs),
        mesh=mesh,
        in_specs=(
            P("grp", "seq", None),
            P("grp", "seq", None),
            P("grp", "seq", None),
            P("grp", "seq", None),
            P(("grp", "seq"), None),
            P("grp"),
            P("grp", None),
        ),
        out_specs=(
            P("grp", "seq", None),
            P("grp", "seq", None),
            P("grp", "seq", None),
            P(("grp", "seq"), None),
        ),
        check_vma=False,
    )
```

```python
import functools
import math

import jax
import jax.numpy as jnp
from jax import lax
from jax.experimental import pallas as pl
from jax.experimental.pallas import tpu as pltpu
from jax.sharding import PartitionSpec as P

MESH = pl.DeviceIdType.MESH
CORES = 2


def place(cols):
    grp = lax.axis_index("grp")
    seq = lax.axis_index("seq")
    return grp, seq, grp // CORES, grp % CORES


def greet(cols, seqs):
    grp, seq, col, core = place(cols)
    barrier = pltpu.get_barrier_semaphore()
    peers = [(grp, (seq + k) % seqs) for k in range(1, seqs)]
    peers += [(((col + j) % cols) * CORES + core, seq) for j in range(1, cols)]
    peers += [(col * CORES + 1 - core, seq)]
    for peer in peers:
        pl.semaphore_signal(barrier, inc=1, device_id=peer, device_id_type=MESH)
    pl.semaphore_wait(barrier, len(peers))


def remote(src, dst, send, recv, device):
    return pltpu.make_async_remote_copy(
        src_ref=src, dst_ref=dst, send_sem=send, recv_sem=recv, device_id=device, device_id_type=MESH
    )


def encode(x, group):
    rows, width = x.shape
    parts = x.reshape(rows // group, group, width)
    top = jnp.maximum(jnp.max(jnp.abs(parts), 1, keepdims=True), 1e-33)
    code = jnp.floor(parts * (32000.0 / top) + 0.5).astype(jnp.int32)
    return code.reshape(rows, width).astype(jnp.int16), (top * (1.0 / 32000.0)).reshape(rows // group, width)


def decode(code, scale):
    rows, width = code.shape
    groups = scale.shape[0]
    parts = code.astype(jnp.int32).astype(jnp.float32).reshape(groups, rows // groups, width)
    return (parts * scale.reshape(groups, 1, width)).reshape(rows, width)


class Pair:
    def __init__(self, codes, scales, sends, recvs, index, device):
        self.copies = [
            remote(src.at[index], dst.at[index], sends.at[i, index], recvs.at[i, index], device)
            for i, (src, dst) in enumerate((codes, scales))
        ]

    def start(self):
        for copy in self.copies:
            copy.start()

    def wait_recv(self):
        for copy in self.copies:
            copy.wait_recv()

    def wait_send(self):
        for copy in self.copies:
            copy.wait_send()


def gather_kernel(cols, seqs, w_ref, out_ref, zs, zr, xs, xr, cs, cr, own_sem):
    grp, seq, col, core = place(cols)
    sibling = (col * CORES + 1 - core, seq)
    greet(cols, seqs)
    own = pltpu.make_async_copy(w_ref.at[0], out_ref.at[grp * seqs + seq], own_sem)
    own.start()
    sent = []
    for k in range(1, seqs):
        copy = remote(
            w_ref.at[0], out_ref.at[grp * seqs + seq], zs.at[k - 1], zr.at[k - 1], (grp, (seq + k) % seqs)
        )
        copy.start()
        sent.append(copy)
    first = list(sent)
    across = {}
    over = []
    for k in range(seqs):
        if k:
            first[k - 1].wait_recv()
        index = grp * seqs + (seq + seqs - k) % seqs
        src = w_ref.at[0] if k == 0 else out_ref.at[index]
        for j in range(1, cols):
            copy = remote(
                src, out_ref.at[index], xs.at[k, j - 1], xr.at[k, j - 1], (((col + j) % cols) * CORES + core, seq)
            )
            copy.start()
            across[k, j] = copy
        copy = remote(src, out_ref.at[index], cs.at[k, 0], cr.at[k, 0], sibling)
        copy.start()
        over.append(copy)
    for k in range(seqs):
        for j in range(1, cols):
            across[k, j].wait_recv()
            index = (((col + cols - j) % cols) * CORES + core) * seqs + (seq + seqs - k) % seqs
            copy = remote(out_ref.at[index], out_ref.at[index], cs.at[k, j], cr.at[k, j], sibling)
            copy.start()
            over.append(copy)
    for copy in over:
        copy.wait_recv()
    for copy in sent + list(across.values()) + over:
        copy.wait_send()
    own.wait()


def gather_weight(weight, cols, seqs):
    rows, width = weight.shape
    out = pl.pallas_call(
        functools.partial(gather_kernel, cols, seqs),
        out_shape=jax.ShapeDtypeStruct((cols * CORES * seqs, rows, width), weight.dtype),
        in_specs=[pl.BlockSpec(memory_space=pl.ANY)],
        out_specs=pl.BlockSpec(memory_space=pl.ANY),
        scratch_shapes=[
            pltpu.SemaphoreType.DMA((seqs - 1,)),
            pltpu.SemaphoreType.DMA((seqs - 1,)),
            pltpu.SemaphoreType.DMA((seqs, cols - 1)),
            pltpu.SemaphoreType.DMA((seqs, cols - 1)),
            pltpu.SemaphoreType.DMA((seqs, cols)),
            pltpu.SemaphoreType.DMA((seqs, cols)),
            pltpu.SemaphoreType.DMA,
        ],
        compiler_params=pltpu.CompilerParams(collective_id=0, has_side_effects=True),
        name="gather_weight",
    )(weight[None])
    return out.reshape(cols * CORES * seqs * rows, width)


def finish_kernel(
    cols, seqs, part_ref, rgrad_ref, x_ref, xr_ref, pgrad_ref, wgrad_ref,
    xbuf, gt, ksend, krecv, kscale, kscaled, pair, crecv, xsend, xrecv, xscale, xscaled,
    total, zsend, zrecv, zscale, zscaled,
    xsem, ks, kr, cs, cr, xs, xr, zs, zr,
):
    grp, seq, col, core = place(cols)
    sibling = (col * CORES + 1 - core, seq)
    plen, width = pgrad_ref.shape
    rt = rgrad_ref.shape[0]
    block = pair.shape[1]
    half = block // CORES
    rows = wgrad_ref.shape[0]
    loads = []
    for j in range(cols):
        at = pl.ds(pl.multiple_of(((col + j) % cols) * block, 128), block)
        loads.append(pltpu.make_async_copy(x_ref.at[:, at], xbuf.at[j, pl.ds(0, plen)], xsem.at[0, j]))
        loads.append(pltpu.make_async_copy(xr_ref.at[:, at], xbuf.at[j, pl.ds(plen, rt)], xsem.at[1, j]))
    for load in loads:
        load.start()
    greet(cols, seqs)

    sends = []
    for k in range(1, seqs):
        for t in range(0, plen, 512):
            ksend[k - 1, pl.ds(t, 512)], kscale[k - 1, pl.ds(t // 64, 8)] = encode(
                part_ref[(seq + k) % seqs, pl.ds(t, 512)], 64
            )
        copy = Pair(
            (ksend, krecv), (kscale, kscaled), ks, kr, k - 1, (grp, (seq + k) % seqs)
        )
        copy.start()
        sends.append(copy)
    gt[:, pl.ds(plen, rt)] = rgrad_ref[...].astype(jnp.float32).T.astype(jnp.bfloat16)
    for load in loads:
        load.wait()
    for copy in sends:
        copy.wait_recv()
    for t in range(0, plen, 512):
        at = pl.ds(t, 512)
        acc = part_ref[seq, at, :]
        for k in range(1, seqs):
            acc = acc + decode(krecv[k - 1, at, :], kscaled[k - 1, pl.ds(t // 64, 8)])
        grad = acc.astype(jnp.bfloat16)
        pgrad_ref[at, :] = grad
        gt[:, at] = grad.astype(jnp.float32).T.astype(jnp.bfloat16)

    tile = 256 if block % 256 == 0 else 128
    mine = pl.ds(pl.multiple_of(core * half, 8), half)
    other = pl.ds(pl.multiple_of((1 - core) * half, 8), half)
    order = list(range(1, cols)) + [0]
    over, across = {}, {}

    def forward(j):
        over[j].wait_recv()
        xsend[j - 1], xscale[j - 1] = encode(pair[j, mine, :] + crecv[j], 64)
        copy = Pair(
            (xsend, xrecv), (xscale, xscaled), xs, xr, j - 1, (((col + j) % cols) * CORES + core, seq)
        )
        copy.start()
        across[j] = copy

    for step, j in enumerate(order):
        for t in range(0, block, tile):
            at = pl.ds(t, tile)
            prod = jnp.dot(gt[...], xbuf[j, :, at], preferred_element_type=jnp.float32)
            pair[j, at, :] = prod.T
        copy = remote(pair.at[j, other], crecv.at[j], cs.at[j], cr.at[j], sibling)
        copy.start()
        over[j] = copy
        if step:
            forward(order[step - 1])
    over[0].wait_recv()
    total[...] = pair[0, mine, :] + crecv[0]
    for j in range(1, cols):
        across[j].wait_recv()
        total[...] += decode(xrecv[j - 1], xscaled[j - 1])

    last = []
    for k in range(1, seqs):
        at = pl.ds(pl.multiple_of(((seq + k) % seqs) * rows, 8), rows)
        zsend[k - 1], zscale[k - 1] = encode(total[at, :], math.gcd(rows, 32))
        copy = Pair(
            (zsend, zrecv), (zscale, zscaled), zs, zr, k - 1, (grp, (seq + k) % seqs)
        )
        copy.start()
        last.append(copy)
    acc = total[pl.ds(pl.multiple_of(seq * rows, 8), rows), :]
    for k in range(1, seqs):
        last[k - 1].wait_recv()
        acc = acc + decode(zrecv[k - 1], zscaled[k - 1])
    wgrad_ref[...] = acc
    for copy in sends + list(over.values()) + list(across.values()) + last:
        copy.wait_send()


def finish(part, rgrad, x, xr, cols, seqs):
    plen, d = x.shape
    rt = xr.shape[0]
    width = part.shape[-1]
    block = d // cols
    half = block // CORES
    rows = half // seqs
    bf16, f32, i16 = jnp.bfloat16, jnp.float32, jnp.int16
    vmem = pl.BlockSpec(memory_space=pltpu.VMEM)
    hbm = pl.BlockSpec(memory_space=pl.ANY)
    dma = pltpu.SemaphoreType.DMA
    return pl.pallas_call(
        functools.partial(finish_kernel, cols, seqs),
        out_shape=(
            jax.ShapeDtypeStruct((plen, width), bf16),
            jax.ShapeDtypeStruct((rows, width), f32),
        ),
        in_specs=[vmem, vmem, hbm, hbm],
        out_specs=(vmem, vmem),
        scratch_shapes=[
            pltpu.VMEM((cols, plen + rt, block), bf16),
            pltpu.VMEM((width, plen + rt), bf16),
            pltpu.VMEM((seqs - 1, plen, width), i16),
            pltpu.VMEM((seqs - 1, plen, width), i16),
            pltpu.VMEM((seqs - 1, plen // 64, width), f32),
            pltpu.VMEM((seqs - 1, plen // 64, width), f32),
            pltpu.VMEM((cols, block, width), f32),
            pltpu.VMEM((cols, half, width), f32),
            pltpu.VMEM((cols - 1, half, width), i16),
            pltpu.VMEM((cols - 1, half, width), i16),
            pltpu.VMEM((cols - 1, half // 64, width), f32),
            pltpu.VMEM((cols - 1, half // 64, width), f32),
            pltpu.VMEM((half, width), f32),
            pltpu.VMEM((seqs - 1, rows, width), i16),
            pltpu.VMEM((seqs - 1, rows, width), i16),
            pltpu.VMEM((seqs - 1, rows // math.gcd(rows, 32), width), f32),
            pltpu.VMEM((seqs - 1, rows // math.gcd(rows, 32), width), f32),
            dma((2, cols)),
            dma((2, seqs - 1)), dma((2, seqs - 1)),
            dma((cols,)), dma((cols,)),
            dma((2, cols - 1)), dma((2, cols - 1)),
            dma((2, seqs - 1)), dma((2, seqs - 1)),
        ],
        compiler_params=pltpu.CompilerParams(
            collective_id=1, has_side_effects=True, vmem_limit_bytes=52 * 2**20
        ),
        name="finish",
    )(part, rgrad, x, xr)


def attend_kernel(
    lens_ref, q_ref, g_ref, kv_ref, rkv_ref, out_ref, qg_ref, part_ref, rgrad_ref, kvt, score, rpart
):
    step = pl.program_id(0)
    f32, bf16 = jnp.float32, jnp.bfloat16
    slots = q_ref.shape[0]
    dim = rkv_ref.shape[1] // 2
    chunk = 512
    chunks = kv_ref.shape[0] // chunk
    scale = dim ** (-0.5)
    prompt_len, resp_len = lens_ref[0], lens_ref[1]

    def rows(c):
        return pl.ds(pl.multiple_of(c * chunk, chunk), chunk)

    @pl.when(step == 0)
    def _():
        def init(c, carry):
            kvt[:, rows(c)] = kv_ref[rows(c), :].T
            part_ref[rows(c), :] = jnp.zeros((chunk, 2 * dim), f32)
            return carry

        lax.fori_loop(0, chunks, init, 0)
        rpart[...] = jnp.zeros_like(rpart)

    q2 = jnp.concatenate([q_ref[:, :dim], q_ref[:, dim:]], 0)
    g2 = jnp.concatenate([g_ref[:, :dim], g_ref[:, dim:]], 0)
    live = lax.broadcasted_iota(jnp.int32, g2.shape, 0) % slots < resp_len
    g32 = jnp.where(live, g2.astype(f32), 0.0)
    g2 = g32.astype(bf16)
    rows_by = (((1,), (1,)), ((), ()))

    def dot_nt(a, b):
        return lax.dot_general(a, b, rows_by, preferred_element_type=f32)

    def dot(a, b):
        return jnp.dot(a, b, preferred_element_type=f32)

    rkeys, rvalues = rkv_ref[:, :dim], rkv_ref[:, dim:]
    rscore = dot_nt(rkeys, q2) * scale
    at_key = lax.broadcasted_iota(jnp.int32, rscore.shape, 0)
    at_slot = lax.broadcasted_iota(jnp.int32, rscore.shape, 1) % slots
    rscore = jnp.where(at_key <= at_slot, rscore, -jnp.inf)

    def scores(c, top):
        s = dot_nt(kv_ref[rows(c), :dim], q2) * scale
        at = lax.broadcasted_iota(jnp.int32, s.shape, 0) + c * chunk
        s = jnp.where(at < prompt_len, s, -jnp.inf)
        score[rows(c), :] = s
        return jnp.maximum(top, jnp.max(s, 0, keepdims=True))

    top = lax.fori_loop(0, chunks, scores, jnp.max(rscore, 0, keepdims=True))
    rexpo = jnp.exp(rscore - top)

    def expos(c, total):
        e = jnp.exp(score[rows(c), :] - top)
        score[rows(c), :] = e
        return total + jnp.sum(e, 0, keepdims=True)

    total = lax.fori_loop(0, chunks, expos, jnp.sum(rexpo, 0, keepdims=True))
    inverse = 1.0 / total
    rprobs_b = (rexpo * inverse).astype(bf16)
    rpart[:, dim:] += dot(rprobs_b, g2)

    def attend(c, acc):
        probs_b = (score[rows(c), :] * inverse).astype(bf16)
        part_ref[rows(c), dim:] += dot(probs_b, g2)
        return acc + dot(kvt[dim:, rows(c)], probs_b)

    acc = lax.fori_loop(0, chunks, attend, dot(rvalues.astype(f32).T.astype(bf16), rprobs_b))
    out = jnp.where(live, acc.T, 0.0).astype(bf16)
    out_ref[...] = jnp.concatenate([out[:slots], out[slots:]], 1)
    delta = jnp.sum(g32.T * out.astype(f32).T, 0, keepdims=True)
    scaled = inverse * scale
    rdscore = (rexpo * scaled * (dot_nt(rvalues, g2) - delta)).astype(bf16)
    rpart[:, :dim] += dot(rdscore, q2)

    def back(c, acc):
        dprob = dot_nt(kv_ref[rows(c), dim:], g2)
        dscore = (score[rows(c), :] * scaled * (dprob - delta)).astype(bf16)
        part_ref[rows(c), :dim] += dot(dscore, q2)
        return acc + dot(kvt[:dim, rows(c)], dscore)

    acc = lax.fori_loop(0, chunks, back, dot(rkeys.astype(f32).T.astype(bf16), rdscore))
    grad = acc.T.astype(bf16)
    qg_ref[...] = jnp.concatenate([grad[:slots], grad[slots:]], 1)
    rgrad_ref[...] = rpart[...].astype(bf16)


def attend(lens, q, g, kv, rkv):
    slots, width = q.shape
    plen, kv_width = kv.shape
    bf16, f32 = jnp.bfloat16, jnp.float32
    heads = pl.BlockSpec((slots, kv_width), lambda i: (0, i))

    def whole(rows):
        return pl.BlockSpec((rows, kv_width), lambda i: (0, 0))

    return pl.pallas_call(
        attend_kernel,
        grid=(width // kv_width,),
        out_shape=(
            jax.ShapeDtypeStruct((slots, width), bf16),
            jax.ShapeDtypeStruct((slots, width), bf16),
            jax.ShapeDtypeStruct((plen, kv_width), f32),
            jax.ShapeDtypeStruct((slots, kv_width), bf16),
        ),
        in_specs=[pl.BlockSpec(memory_space=pltpu.SMEM), heads, heads, whole(plen), whole(slots)],
        out_specs=(heads, heads, whole(plen), whole(slots)),
        scratch_shapes=[
            pltpu.VMEM((kv_width, plen), bf16),
            pltpu.VMEM((plen, 2 * slots), f32),
            pltpu.VMEM((slots, kv_width), f32),
        ],
        compiler_params=pltpu.CompilerParams(vmem_limit_bytes=52 * 2**20),
        name="attend",
    )(lens, q, g, kv, rkv)


def per_device(
    cols, seqs,
    prompt_hidden, resp_hidden, queries, grad_out, kv_weight, prompt_lengths, response_lengths
):
    seq_rank = lax.axis_index("seq")
    prompt_rows = prompt_hidden[0]
    resp_rows = resp_hidden[0]
    piece = gather_weight(kv_weight, cols, seqs)
    own_kv = jnp.dot(prompt_rows, piece, preferred_element_type=jnp.float32).astype(jnp.bfloat16)
    resp_kv = jnp.dot(resp_rows, piece, preferred_element_type=jnp.float32).astype(jnp.bfloat16)
    prompt_kv = lax.all_gather(own_kv, "seq", axis=0, tiled=True)
    members = jnp.arange(response_lengths.shape[1])
    resp_len = jnp.sum(jnp.where(members == seq_rank, response_lengths[0], 0))
    lens = jnp.stack([prompt_lengths[0], resp_len])
    attended, query_grad, part, resp_grad = attend(lens, queries[0], grad_out[0], prompt_kv, resp_kv)
    part = part.reshape(seqs, part.shape[0] // seqs, part.shape[1])
    prompt_grad, weight_grad = finish(part, resp_grad, prompt_rows, resp_rows, cols, seqs)
    return (attended[None], query_grad[None], prompt_grad[None], weight_grad)


def solution(mesh):
    cols, seqs = mesh.shape["grp"] // CORES, mesh.shape["seq"]
    return jax.shard_map(
        functools.partial(per_device, cols, seqs),
        mesh=mesh,
        in_specs=(
            P("grp", "seq", None),
            P("grp", "seq", None),
            P("grp", "seq", None),
            P("grp", "seq", None),
            P(("grp", "seq"), None),
            P("grp"),
            P("grp", None),
        ),
        out_specs=(
            P("grp", "seq", None),
            P("grp", "seq", None),
            P("grp", "seq", None),
            P(("grp", "seq"), None),
        ),
        check_vma=False,
    )
```

```python
import functools
import math

import jax
import jax.numpy as jnp
from jax import lax
from jax.experimental import pallas as pl
from jax.experimental.pallas import tpu as pltpu
from jax.sharding import PartitionSpec as P

MESH = pl.DeviceIdType.MESH
CORES = 2


def place(cols):
    grp = lax.axis_index("grp")
    seq = lax.axis_index("seq")
    return grp, seq, grp // CORES, grp % CORES


def greet(cols, seqs):
    grp, seq, col, core = place(cols)
    barrier = pltpu.get_barrier_semaphore()
    peers = [(grp, (seq + k) % seqs) for k in range(1, seqs)]
    peers += [(((col + j) % cols) * CORES + core, seq) for j in range(1, cols)]
    peers += [(col * CORES + 1 - core, seq)]
    for peer in peers:
        pl.semaphore_signal(barrier, inc=1, device_id=peer, device_id_type=MESH)
    pl.semaphore_wait(barrier, len(peers))


def remote(src, dst, send, recv, device):
    return pltpu.make_async_remote_copy(
        src_ref=src, dst_ref=dst, send_sem=send, recv_sem=recv, device_id=device, device_id_type=MESH
    )


def encode(x, group):
    rows, width = x.shape
    parts = x.reshape(rows // group, group, width)
    top = jnp.maximum(jnp.max(jnp.abs(parts), 1, keepdims=True), 1e-33)
    code = jnp.floor(parts * (32000.0 / top) + 0.5).astype(jnp.int32)
    return code.reshape(rows, width).astype(jnp.int16), (top * (1.0 / 32000.0)).reshape(rows // group, width)


def decode(code, scale):
    rows, width = code.shape
    groups = scale.shape[0]
    parts = code.astype(jnp.int32).astype(jnp.float32).reshape(groups, rows // groups, width)
    return (parts * scale.reshape(groups, 1, width)).reshape(rows, width)


class Pair:
    def __init__(self, codes, scales, sends, recvs, index, device):
        self.copies = [
            remote(src.at[index], dst.at[index], sends.at[i, index], recvs.at[i, index], device)
            for i, (src, dst) in enumerate((codes, scales))
        ]

    def start(self):
        for copy in self.copies:
            copy.start()

    def wait_recv(self):
        for copy in self.copies:
            copy.wait_recv()

    def wait_send(self):
        for copy in self.copies:
            copy.wait_send()


def gather_kernel(cols, seqs, w_ref, out_ref, zs, zr, xs, xr, cs, cr, own_sem):
    grp, seq, col, core = place(cols)
    sibling = (col * CORES + 1 - core, seq)
    greet(cols, seqs)
    own = pltpu.make_async_copy(w_ref.at[0], out_ref.at[grp * seqs + seq], own_sem)
    own.start()
    sent = []
    for k in range(1, seqs):
        copy = remote(
            w_ref.at[0], out_ref.at[grp * seqs + seq], zs.at[k - 1], zr.at[k - 1], (grp, (seq + k) % seqs)
        )
        copy.start()
        sent.append(copy)
    first = list(sent)
    across = {}
    over = []
    for k in range(seqs):
        if k:
            first[k - 1].wait_recv()
        index = grp * seqs + (seq + seqs - k) % seqs
        src = w_ref.at[0] if k == 0 else out_ref.at[index]
        for j in range(1, cols):
            copy = remote(
                src, out_ref.at[index], xs.at[k, j - 1], xr.at[k, j - 1], (((col + j) % cols) * CORES + core, seq)
            )
            copy.start()
            across[k, j] = copy
        copy = remote(src, out_ref.at[index], cs.at[k, 0], cr.at[k, 0], sibling)
        copy.start()
        over.append(copy)
    for k in range(seqs):
        for j in range(1, cols):
            across[k, j].wait_recv()
            index = (((col + cols - j) % cols) * CORES + core) * seqs + (seq + seqs - k) % seqs
            copy = remote(out_ref.at[index], out_ref.at[index], cs.at[k, j], cr.at[k, j], sibling)
            copy.start()
            over.append(copy)
    for copy in over:
        copy.wait_recv()
    for copy in sent + list(across.values()) + over:
        copy.wait_send()
    own.wait()


def gather_weight(weight, cols, seqs):
    rows, width = weight.shape
    out = pl.pallas_call(
        functools.partial(gather_kernel, cols, seqs),
        out_shape=jax.ShapeDtypeStruct((cols * CORES * seqs, rows, width), weight.dtype),
        in_specs=[pl.BlockSpec(memory_space=pl.ANY)],
        out_specs=pl.BlockSpec(memory_space=pl.ANY),
        scratch_shapes=[
            pltpu.SemaphoreType.DMA((seqs - 1,)),
            pltpu.SemaphoreType.DMA((seqs - 1,)),
            pltpu.SemaphoreType.DMA((seqs, cols - 1)),
            pltpu.SemaphoreType.DMA((seqs, cols - 1)),
            pltpu.SemaphoreType.DMA((seqs, cols)),
            pltpu.SemaphoreType.DMA((seqs, cols)),
            pltpu.SemaphoreType.DMA,
        ],
        compiler_params=pltpu.CompilerParams(collective_id=0, has_side_effects=True),
        name="gather_weight",
    )(weight[None])
    return out.reshape(cols * CORES * seqs * rows, width)


def finish_kernel(
    cols, seqs, part_ref, rgrad_ref, x_ref, xr_ref, pgrad_ref, wgrad_ref,
    xbuf, gt, ksend, krecv, kscale, kscaled, pair, crecv, xsend, xrecv, xscale, xscaled,
    total, zsend, zrecv, zscale, zscaled,
    xsem, ks, kr, cs, cr, xs, xr, zs, zr,
):
    grp, seq, col, core = place(cols)
    sibling = (col * CORES + 1 - core, seq)
    plen, width = pgrad_ref.shape
    rt = rgrad_ref.shape[0]
    block = pair.shape[1]
    half = block // CORES
    rows = wgrad_ref.shape[0]
    loads = []
    for j in range(cols):
        at = pl.ds(pl.multiple_of(((col + j) % cols) * block, 128), block)
        loads.append(pltpu.make_async_copy(x_ref.at[:, at], xbuf.at[j, pl.ds(0, plen)], xsem.at[0, j]))
        loads.append(pltpu.make_async_copy(xr_ref.at[:, at], xbuf.at[j, pl.ds(plen, rt)], xsem.at[1, j]))
    for load in loads:
        load.start()
    greet(cols, seqs)

    sends = []
    for k in range(1, seqs):
        for t in range(0, plen, 512):
            ksend[k - 1, pl.ds(t, 512)], kscale[k - 1, pl.ds(t // 64, 8)] = encode(
                part_ref[(seq + k) % seqs, pl.ds(t, 512)], 64
            )
        copy = Pair(
            (ksend, krecv), (kscale, kscaled), ks, kr, k - 1, (grp, (seq + k) % seqs)
        )
        copy.start()
        sends.append(copy)
    gt[:, pl.ds(plen, rt)] = rgrad_ref[...].astype(jnp.float32).T.astype(jnp.bfloat16)
    for load in loads:
        load.wait()
    for copy in sends:
        copy.wait_recv()
    for t in range(0, plen, 512):
        at = pl.ds(t, 512)
        acc = part_ref[seq, at, :]
        for k in range(1, seqs):
            acc = acc + decode(krecv[k - 1, at, :], kscaled[k - 1, pl.ds(t // 64, 8)])
        grad = acc.astype(jnp.bfloat16)
        pgrad_ref[at, :] = grad
        gt[:, at] = grad.astype(jnp.float32).T.astype(jnp.bfloat16)

    tile = 256 if block % 256 == 0 else 128
    mine = pl.ds(pl.multiple_of(core * half, 8), half)
    other = pl.ds(pl.multiple_of((1 - core) * half, 8), half)
    order = list(range(1, cols)) + [0]
    over, across = {}, {}

    def forward(j):
        over[j].wait_recv()
        xsend[j - 1], xscale[j - 1] = encode(pair[j, mine, :] + crecv[j], 64)
        copy = Pair(
            (xsend, xrecv), (xscale, xscaled), xs, xr, j - 1, (((col + j) % cols) * CORES + core, seq)
        )
        copy.start()
        across[j] = copy

    for step, j in enumerate(order):
        for t in range(0, block, tile):
            at = pl.ds(t, tile)
            prod = jnp.dot(gt[...], xbuf[j, :, at], preferred_element_type=jnp.float32)
            pair[j, at, :] = prod.T
        copy = remote(pair.at[j, other], crecv.at[j], cs.at[j], cr.at[j], sibling)
        copy.start()
        over[j] = copy
        if step:
            forward(order[step - 1])
    over[0].wait_recv()
    total[...] = pair[0, mine, :] + crecv[0]
    for j in range(1, cols):
        across[j].wait_recv()
        total[...] += decode(xrecv[j - 1], xscaled[j - 1])

    last = []
    for k in range(1, seqs):
        at = pl.ds(pl.multiple_of(((seq + k) % seqs) * rows, 8), rows)
        zsend[k - 1], zscale[k - 1] = encode(total[at, :], math.gcd(rows, 32))
        copy = Pair(
            (zsend, zrecv), (zscale, zscaled), zs, zr, k - 1, (grp, (seq + k) % seqs)
        )
        copy.start()
        last.append(copy)
    acc = total[pl.ds(pl.multiple_of(seq * rows, 8), rows), :]
    for k in range(1, seqs):
        last[k - 1].wait_recv()
        acc = acc + decode(zrecv[k - 1], zscaled[k - 1])
    wgrad_ref[...] = acc
    for copy in sends + list(over.values()) + list(across.values()) + last:
        copy.wait_send()


def finish(part, rgrad, x, xr, cols, seqs):
    plen, d = x.shape
    rt = xr.shape[0]
    width = part.shape[-1]
    block = d // cols
    half = block // CORES
    rows = half // seqs
    bf16, f32, i16 = jnp.bfloat16, jnp.float32, jnp.int16
    vmem = pl.BlockSpec(memory_space=pltpu.VMEM)
    hbm = pl.BlockSpec(memory_space=pl.ANY)
    dma = pltpu.SemaphoreType.DMA
    return pl.pallas_call(
        functools.partial(finish_kernel, cols, seqs),
        out_shape=(
            jax.ShapeDtypeStruct((plen, width), bf16),
            jax.ShapeDtypeStruct((rows, width), f32),
        ),
        in_specs=[vmem, vmem, hbm, hbm],
        out_specs=(vmem, vmem),
        scratch_shapes=[
            pltpu.VMEM((cols, plen + rt, block), bf16),
            pltpu.VMEM((width, plen + rt), bf16),
            pltpu.VMEM((seqs - 1, plen, width), i16),
            pltpu.VMEM((seqs - 1, plen, width), i16),
            pltpu.VMEM((seqs - 1, plen // 64, width), f32),
            pltpu.VMEM((seqs - 1, plen // 64, width), f32),
            pltpu.VMEM((cols, block, width), f32),
            pltpu.VMEM((cols, half, width), f32),
            pltpu.VMEM((cols - 1, half, width), i16),
            pltpu.VMEM((cols - 1, half, width), i16),
            pltpu.VMEM((cols - 1, half // 64, width), f32),
            pltpu.VMEM((cols - 1, half // 64, width), f32),
            pltpu.VMEM((half, width), f32),
            pltpu.VMEM((seqs - 1, rows, width), i16),
            pltpu.VMEM((seqs - 1, rows, width), i16),
            pltpu.VMEM((seqs - 1, rows // math.gcd(rows, 32), width), f32),
            pltpu.VMEM((seqs - 1, rows // math.gcd(rows, 32), width), f32),
            dma((2, cols)),
            dma((2, seqs - 1)), dma((2, seqs - 1)),
            dma((cols,)), dma((cols,)),
            dma((2, cols - 1)), dma((2, cols - 1)),
            dma((2, seqs - 1)), dma((2, seqs - 1)),
        ],
        compiler_params=pltpu.CompilerParams(
            collective_id=1, has_side_effects=True, vmem_limit_bytes=52 * 2**20
        ),
        name="finish",
    )(part, rgrad, x, xr)


def attend_kernel(
    lens_ref, q_ref, g_ref, kv_ref, rkv_ref, out_ref, qg_ref, part_ref, rgrad_ref, kvt, score, rpart
):
    step = pl.program_id(0)
    f32, bf16 = jnp.float32, jnp.bfloat16
    slots = q_ref.shape[0]
    dim = rkv_ref.shape[1] // 2
    chunk = 512
    chunks = kv_ref.shape[0] // chunk
    scale = dim ** (-0.5)
    prompt_len, resp_len = lens_ref[0], lens_ref[1]

    def rows(c):
        return pl.ds(pl.multiple_of(c * chunk, chunk), chunk)

    @pl.when(step == 0)
    def _():
        def init(c, carry):
            kvt[:, rows(c)] = kv_ref[rows(c), :].T
            part_ref[rows(c), :] = jnp.zeros((chunk, 2 * dim), f32)
            return carry

        lax.fori_loop(0, chunks, init, 0)
        rpart[...] = jnp.zeros_like(rpart)

    q2 = jnp.concatenate([q_ref[:, :dim], q_ref[:, dim:]], 0)
    g2 = jnp.concatenate([g_ref[:, :dim], g_ref[:, dim:]], 0)
    live = lax.broadcasted_iota(jnp.int32, g2.shape, 0) % slots < resp_len
    g32 = jnp.where(live, g2.astype(f32), 0.0)
    g2 = g32.astype(bf16)
    rows_by = (((1,), (1,)), ((), ()))

    def dot_nt(a, b):
        return lax.dot_general(a, b, rows_by, preferred_element_type=f32)

    def dot(a, b):
        return jnp.dot(a, b, preferred_element_type=f32)

    rkeys, rvalues = rkv_ref[:, :dim], rkv_ref[:, dim:]
    rscore = dot_nt(rkeys, q2) * scale
    at_key = lax.broadcasted_iota(jnp.int32, rscore.shape, 0)
    at_slot = lax.broadcasted_iota(jnp.int32, rscore.shape, 1) % slots
    rscore = jnp.where(at_key <= at_slot, rscore, -jnp.inf)

    def scores(c, top):
        s = dot_nt(kv_ref[rows(c), :dim], q2) * scale
        at = lax.broadcasted_iota(jnp.int32, s.shape, 0) + c * chunk
        s = jnp.where(at < prompt_len, s, -jnp.inf)
        score[rows(c), :] = s
        return jnp.maximum(top, jnp.max(s, 0, keepdims=True))

    top = lax.fori_loop(0, chunks, scores, jnp.max(rscore, 0, keepdims=True), unroll=4)
    rexpo = jnp.exp(rscore - top)

    def expos(c, total):
        e = jnp.exp(score[rows(c), :] - top)
        score[rows(c), :] = e
        return total + jnp.sum(e, 0, keepdims=True)

    total = lax.fori_loop(0, chunks, expos, jnp.sum(rexpo, 0, keepdims=True), unroll=4)
    inverse = 1.0 / total
    rprobs_b = (rexpo * inverse).astype(bf16)
    rpart[:, dim:] += dot(rprobs_b, g2)

    def attend(c, acc):
        probs_b = (score[rows(c), :] * inverse).astype(bf16)
        part_ref[rows(c), dim:] += dot(probs_b, g2)
        return acc + dot(kvt[dim:, rows(c)], probs_b)

    acc = lax.fori_loop(0, chunks, attend, dot(rvalues.astype(f32).T.astype(bf16), rprobs_b), unroll=4)
    out = jnp.where(live, acc.T, 0.0).astype(bf16)
    out_ref[...] = jnp.concatenate([out[:slots], out[slots:]], 1)
    delta = jnp.sum(g32.T * out.astype(f32).T, 0, keepdims=True)
    scaled = inverse * scale
    rdscore = (rexpo * scaled * (dot_nt(rvalues, g2) - delta)).astype(bf16)
    rpart[:, :dim] += dot(rdscore, q2)

    def back(c, acc):
        dprob = dot_nt(kv_ref[rows(c), dim:], g2)
        dscore = (score[rows(c), :] * scaled * (dprob - delta)).astype(bf16)
        part_ref[rows(c), :dim] += dot(dscore, q2)
        return acc + dot(kvt[:dim, rows(c)], dscore)

    acc = lax.fori_loop(0, chunks, back, dot(rkeys.astype(f32).T.astype(bf16), rdscore), unroll=4)
    grad = acc.T.astype(bf16)
    qg_ref[...] = jnp.concatenate([grad[:slots], grad[slots:]], 1)
    rgrad_ref[...] = rpart[...].astype(bf16)


def attend(lens, q, g, kv, rkv):
    slots, width = q.shape
    plen, kv_width = kv.shape
    bf16, f32 = jnp.bfloat16, jnp.float32
    heads = pl.BlockSpec((slots, kv_width), lambda i: (0, i))

    def whole(rows):
        return pl.BlockSpec((rows, kv_width), lambda i: (0, 0))

    return pl.pallas_call(
        attend_kernel,
        grid=(width // kv_width,),
        out_shape=(
            jax.ShapeDtypeStruct((slots, width), bf16),
            jax.ShapeDtypeStruct((slots, width), bf16),
            jax.ShapeDtypeStruct((plen, kv_width), f32),
            jax.ShapeDtypeStruct((slots, kv_width), bf16),
        ),
        in_specs=[pl.BlockSpec(memory_space=pltpu.SMEM), heads, heads, whole(plen), whole(slots)],
        out_specs=(heads, heads, whole(plen), whole(slots)),
        scratch_shapes=[
            pltpu.VMEM((kv_width, plen), bf16),
            pltpu.VMEM((plen, 2 * slots), f32),
            pltpu.VMEM((slots, kv_width), f32),
        ],
        compiler_params=pltpu.CompilerParams(vmem_limit_bytes=52 * 2**20),
        name="attend",
    )(lens, q, g, kv, rkv)


def per_device(
    cols, seqs,
    prompt_hidden, resp_hidden, queries, grad_out, kv_weight, prompt_lengths, response_lengths
):
    seq_rank = lax.axis_index("seq")
    prompt_rows = prompt_hidden[0]
    resp_rows = resp_hidden[0]
    piece = gather_weight(kv_weight, cols, seqs)
    own_kv = jnp.dot(prompt_rows, piece, preferred_element_type=jnp.float32).astype(jnp.bfloat16)
    resp_kv = jnp.dot(resp_rows, piece, preferred_element_type=jnp.float32).astype(jnp.bfloat16)
    prompt_kv = lax.all_gather(own_kv, "seq", axis=0, tiled=True)
    members = jnp.arange(response_lengths.shape[1])
    resp_len = jnp.sum(jnp.where(members == seq_rank, response_lengths[0], 0))
    lens = jnp.stack([prompt_lengths[0], resp_len])
    attended, query_grad, part, resp_grad = attend(lens, queries[0], grad_out[0], prompt_kv, resp_kv)
    part = part.reshape(seqs, part.shape[0] // seqs, part.shape[1])
    prompt_grad, weight_grad = finish(part, resp_grad, prompt_rows, resp_rows, cols, seqs)
    return (attended[None], query_grad[None], prompt_grad[None], weight_grad)


def solution(mesh):
    cols, seqs = mesh.shape["grp"] // CORES, mesh.shape["seq"]
    return jax.shard_map(
        functools.partial(per_device, cols, seqs),
        mesh=mesh,
        in_specs=(
            P("grp", "seq", None),
            P("grp", "seq", None),
            P("grp", "seq", None),
            P("grp", "seq", None),
            P(("grp", "seq"), None),
            P("grp"),
            P("grp", None),
        ),
        out_specs=(
            P("grp", "seq", None),
            P("grp", "seq", None),
            P("grp", "seq", None),
            P(("grp", "seq"), None),
        ),
        check_vma=False,
    )
```
